256 devices in a mesh: learn: 8 (over z_hi, x), tp: 16 (over y, z_lo), dp: 2 (over core).
Axes of the slice: x: 4, y: 4, z: 8 (z_hi: 2, z_lo: 4; z = z_hi * 4 + z_lo), core: 2. Of those that a mesh axis runs over, the one named last changes fastest.
Arguments:
- gradient: bfloat16 [29568, 8192], P('tp', ('learn', 'dp')), may hold values from -6 to 6
- frame_basis: bfloat16 [8192, 1024], P(('learn', 'dp')), may hold values from -0.0625 to 0.0625
- moment_first: float32 [29568, 1024], P('tp', ('learn', 'dp')), may hold values from -3 to 3
- moment_second: float32 [29568, 1024], P('tp', ('learn', 'dp')), may hold values from 0.05 to 1
- refresh: int32 [1024], P(('learn', 'dp')), may hold values 0 or 1
- old_weight: bfloat16 [29568, 8192], P('tp', ('learn', 'dp')), may hold values from -0.03125 to 0.03125
- hidden: bfloat16 [128, 29568], P('dp', 'tp'), may hold values from -6 to 6
Outputs:
- new_first: float32 [29568, 1024], P('tp', ('learn', 'dp'))
- new_second: float32 [29568, 1024], P('tp', ('learn', 'dp'))
- new_weight: bfloat16 [29568, 8192], P('tp', ('learn', 'dp'))
- mlp_out: bfloat16 [128, 8192], P('dp', ('learn', 'tp'))
The draws below stay inside these ranges and needn't reach their ends.
All inputs are finite; a program needn't handle non-finite values. No bound on the sum of `refresh` on one device may be relied on, other than what follows from the above.
Results may differ from the reference program's by a relative error of at most 0.0075.
Values may be sent and summed in bfloat16 or wider, within the bound.
No kernel may reach another device: no remote copies, remote signals or barrier semaphores. Data moves between devices by JAX's collectives and lax.ppermute only.
A program may use at most 64 MiB of HBM per device.

```python
import math
import jax
import jax.numpy as jnp
from jax import lax

D = 8192
FF = 29568
RANK = 1024
SEQS = 128
N_TP = 16


def plant(drawn, key, least, largest):
    extent = drawn.shape
    index_at = [jax.random.randint(jax.random.fold_in(key, axis), (), 0, extent[axis]) for axis in range(len(extent))]
    drawn = drawn.at[tuple(index_at)].set(least)
    longest = extent.index(max(extent))
    index_at[longest] = (index_at[longest] + 1) % extent[longest]
    return drawn.at[tuple(index_at)].set(largest)


def block_scale(stream_key, dims, cuts, smallest, high):
    level = 1.0
    for position, blocks in cuts:
        draws = jax.random.uniform(jax.random.fold_in(jax.random.fold_in(stream_key, 6), position), (blocks,), jnp.float32, smallest / len(cuts), high / len(cuts))
        level = level * jnp.repeat(jnp.exp(draws), dims[position] // blocks).reshape((-1,) + (1,) * (len(dims) - 1 - position))
    return level


def normal_values(stream_key, shape, scale, most, shards=(), kind=jnp.bfloat16):
    entries = jax.random.normal(stream_key, shape, jnp.float32) * scale
    if len(shards) > 0:
        entries = block_scale(stream_key, shape, shards, -0.22, 0.18) * entries
    return jnp.clip(entries, min=-most, max=most).astype(kind)


def setup_inputs(seed: int = 0) -> dict:
    splits = jax.random.split(jax.random.key(seed), 8)
    gradient = normal_values(splits[0], (FF, D), 1.0, 6.0, ((0, 16), (1, 16)))
    frame_basis = normal_values(splits[1], (D, RANK), D ** -0.5, 0.0625, ((0, 16),))
    moment_first = normal_values(splits[2], (FF, RANK), 0.5, 3.0, ((0, 16), (1, 16)), jnp.float32)
    moment_second = jnp.clip(jnp.exp(math.log(1.0) - 2.9957323 * jax.random.uniform(splits[3], (FF, RANK), jnp.float32) ** block_scale(splits[3], (FF, RANK), ((0, 16), (1, 16)), -0.2, 0.2)), 0.05, 1.0)
    refresh = plant((jax.random.randint(splits[4], (RANK,), 0, 4) < 1).astype(jnp.int32), jax.random.fold_in(splits[4], 1), 0, 1)
    old_weight = normal_values(splits[5], (FF, D), FF ** -0.5, 0.03125, ((0, 16), (1, 16)))
    hidden = normal_values(splits[6], (SEQS, FF), 1.0, 6.0, ((0, 2), (1, 16)))
    return dict(gradient=gradient, frame_basis=frame_basis, moment_first=moment_first, moment_second=moment_second, refresh=refresh, old_weight=old_weight, hidden=hidden)


BETA_ONE = 0.9
BETA_TWO = 0.999
ADAM_EPS = 1e-06
STEP_RATE = 0.01

def reference(gradient, frame_basis, moment_first, moment_second, refresh, old_weight, hidden):
    projected = jnp.dot(gradient, frame_basis, preferred_element_type=jnp.float32)
    fresh = (refresh == 1)[None, :]
    start_first = jnp.where(fresh, jnp.float32(0.0), moment_first)
    start_second = jnp.where(fresh, jnp.float32(0.0), moment_second)
    new_first = BETA_ONE * start_first + (1.0 - BETA_ONE) * projected
    new_second = BETA_TWO * start_second + (1.0 - BETA_TWO) * projected * projected
    ratio = (new_first / (jnp.sqrt(new_second) + ADAM_EPS)).astype(jnp.bfloat16)
    block_count = N_TP
    block_rows = FF // block_count

    def one_block(block_index):
        first_row = (block_index * block_rows).astype(jnp.int32)
        ratio_rows = lax.dynamic_slice_in_dim(ratio, first_row, block_rows, 0)
        weight_rows = lax.dynamic_slice_in_dim(old_weight, first_row, block_rows, 0)
        delta = jnp.dot(ratio_rows, frame_basis.T, preferred_element_type=jnp.float32)
        block_weight = (weight_rows.astype(jnp.float32) - STEP_RATE * delta).astype(jnp.bfloat16)
        hidden_cols = lax.dynamic_slice_in_dim(hidden, first_row, block_rows, 1)
        return (jnp.dot(hidden_cols, block_weight, preferred_element_type=jnp.float32), block_weight)
    partials, weight_blocks = lax.map(one_block, jnp.arange(block_count, dtype=jnp.int32))
    new_weight = weight_blocks.reshape(FF, D)
    mlp_out = lax.optimization_barrier(jnp.sum(partials, axis=0)).astype(jnp.bfloat16)
    return (new_first, new_second, new_weight, mlp_out)
```

```python
import functools

import jax
import jax.numpy as jnp
from jax import lax
from jax.experimental import pallas as pl
from jax.experimental.pallas import tpu as pltpu
from jax.sharding import PartitionSpec as P

BETA_ONE = 0.9
BETA_TWO = 0.999
ADAM_EPS = 1e-06
STEP_RATE = 0.01
RING = 4
CHUNKS = 2
ROWS = 256
F32 = jnp.float32
BF16 = jnp.bfloat16


def arrange_kernel(where_ref, basis_ref, own_ref, other_ref, turned):
    zh, x, d = where_ref[0], where_ref[1], where_ref[2]
    width = turned.shape[0] // 16
    turned[...] = basis_ref[...].T
    for side, out_ref in ((0, own_ref), (1, other_ref)):
        for j in range(RING):
            for zrel in range(2):
                block = ((zh ^ zrel) * RING + ((x + j) & (RING - 1))) * 2 + (d ^ side)
                first = (2 * j + zrel) * width
                out_ref[first : first + width, :] = turned[
                    pl.ds(pl.multiple_of(block * width, width), width), :
                ]


def arrange(where, basis):
    depth, rank = basis.shape
    out = jax.ShapeDtypeStruct((rank // 2, depth), basis.dtype)
    return pl.pallas_call(
        arrange_kernel,
        grid_spec=pltpu.PrefetchScalarGridSpec(
            num_scalar_prefetch=1,
            grid=(1,),
            in_specs=[pl.BlockSpec((depth, rank), lambda i, w: (0, 0))],
            out_specs=[pl.BlockSpec((rank // 2, depth), lambda i, w: (0, 0))] * 2,
            scratch_shapes=[pltpu.VMEM((rank, depth), basis.dtype)],
        ),
        out_shape=(out, out),
        cost_estimate=pl.CostEstimate(flops=0, bytes_accessed=8 * depth * rank, transcendentals=0),
    )(where, basis)


def project_kernel(own_ref, other_ref, mine_ref, theirs_ref, *outs):
    contract = (((1,), (1,)), ((), ()))
    low = lax.dot_general(own_ref[...], mine_ref[...], contract, preferred_element_type=F32)
    low += lax.dot_general(other_ref[...], theirs_ref[...], contract, preferred_element_type=F32)
    width = low.shape[0] // 8
    for k, out_ref in enumerate(outs):
        out_ref[...] = low[k * width : (k + 1) * width].astype(out_ref.dtype)


def project(basis_own, basis_other, gradient, theirs, first, count):
    ranks, depth = basis_own.shape
    width = ranks // 8
    steps = pl.cdiv(count, ROWS)
    start = first // ROWS
    return pl.pallas_call(
        project_kernel,
        grid=(steps,),
        in_specs=[
            pl.BlockSpec((ranks, depth), lambda i: (0, 0)),
            pl.BlockSpec((ranks, depth), lambda i: (0, 0)),
            pl.BlockSpec((ROWS, depth), lambda i: (start + i, 0)),
            pl.BlockSpec((ROWS, depth), lambda i: (i, 0)),
        ],
        out_specs=[pl.BlockSpec((width, ROWS), lambda i: (0, i))] * 8,
        out_shape=[
            jax.ShapeDtypeStruct((width, count), F32) for k in range(8)
        ],
        cost_estimate=pl.CostEstimate(
            flops=4 * ranks * depth * count, bytes_accessed=8 * depth * count, transcendentals=0
        ),
    )(basis_own, basis_other, gradient, theirs)


def update_kernel(first, limit, has_weight, *refs):
    if has_weight:
        refs = refs[1:]
    (mine_ref, theirs_ref, own_ref, other_ref, old_ref, hid_ref, hid_far_ref, sum_ref, new_ref, out_ref) = refs
    i = pl.program_id(0)
    contract = (((0,), (0,)), ((), ()))
    delta = lax.dot_general(mine_ref[...], own_ref[...], contract, preferred_element_type=F32)
    delta += lax.dot_general(theirs_ref[...], other_ref[...], contract, preferred_element_type=F32)
    new = (old_ref[...].astype(F32) - STEP_RATE * delta).astype(BF16)
    new_ref[...] = new
    left = limit - first - i * ROWS
    new = jnp.where(lax.broadcasted_iota(jnp.int32, new.shape, 0) < left, new, jnp.zeros_like(new))
    hid = jnp.concatenate([hid_ref[...], hid_far_ref[...]], axis=0)
    hid = jnp.where(lax.broadcasted_iota(jnp.int32, hid.shape, 1) < left, hid, jnp.zeros_like(hid))

    @pl.when(i == 0)
    def _():
        out_ref[...] = sum_ref[...]

    out_ref[...] += jnp.dot(hid, new, preferred_element_type=F32)


def update(weight, mine, theirs, basis_own, basis_other, old, hid, hid_far, total, first, count):
    ranks, depth = basis_own.shape
    rows = old.shape[0]
    seqs = hid.shape[0]
    steps = pl.cdiv(count, ROWS)
    start = first // ROWS
    in_specs = [
        pl.BlockSpec((ranks, ROWS), lambda i: (0, i)),
        pl.BlockSpec((ranks, ROWS), lambda i: (0, i)),
        pl.BlockSpec((ranks, depth), lambda i: (0, 0)),
        pl.BlockSpec((ranks, depth), lambda i: (0, 0)),
        pl.BlockSpec((ROWS, depth), lambda i: (start + i, 0)),
        pl.BlockSpec((seqs, ROWS), lambda i: (0, start + i)),
        pl.BlockSpec((seqs, ROWS), lambda i: (0, start + i)),
        pl.BlockSpec((2 * seqs, depth), lambda i: (0, 0)),
    ]
    args = (mine, theirs, basis_own, basis_other, old, hid, hid_far, total)
    aliases = {}
    if weight is not None:
        in_specs = [pl.BlockSpec(memory_space=pl.ANY)] + in_specs
        args = (weight,) + args
        aliases = {0: 0}
    return pl.pallas_call(
        functools.partial(update_kernel, first, rows, weight is not None),
        grid=(steps,),
        in_specs=in_specs,
        out_specs=[
            pl.BlockSpec((ROWS, depth), lambda i: (start + i, 0)),
            pl.BlockSpec((2 * seqs, depth), lambda i: (0, 0)),
        ],
        out_shape=[
            jax.ShapeDtypeStruct((rows, depth), BF16),
            jax.ShapeDtypeStruct((2 * seqs, depth), F32),
        ],
        input_output_aliases=aliases,
        cost_estimate=pl.CostEstimate(
            flops=4 * ranks * depth * count, bytes_accessed=8 * depth * count, transcendentals=0
        ),
    )(*args)


def shards(gradient, frame_basis, moment_first, moment_second, refresh, old_weight, hidden):
    learn = lax.axis_index("learn")
    where = jnp.stack([learn // RING, learn % RING, lax.axis_index("dp")]).astype(jnp.int32)
    up = [(z * RING + x, z * RING + (x + 1) % RING) for z in range(2) for x in range(RING)]
    down = [(b, a) for a, b in up]
    across = [(i, (i + RING) % (2 * RING)) for i in range(2 * RING)]
    plus = lambda v: lax.ppermute(v, "learn", up)
    minus = lambda v: lax.ppermute(v, "learn", down)
    far = lambda v: lax.ppermute(v, "learn", across)
    twin = lambda v: lax.ppermute(v, "dp", [(0, 1), (1, 0)])

    rows = gradient.shape[0]
    size = -(-rows // (CHUNKS * ROWS)) * ROWS
    cuts = [(a, min(size, rows - a)) for a in range(0, rows, size)]

    basis_own, basis_send = arrange(where, frame_basis)
    basis_recv = twin(basis_send)
    hid_far = twin(hidden)
    first_t, second_t = moment_first.T, moment_second.T
    fresh = (refresh == 1)[:, None]

    ratios = []
    firsts, seconds = [], []
    for a, n in cuts:
        theirs = twin(gradient[a : a + n])
        p00, p01, p10, p11, p20, p21, p30, p31 = project(basis_own, basis_recv, gradient, theirs, a, n)
        from_low = plus(p20)
        from_high = minus(p21)
        low1 = plus(p11)
        high0 = minus(p30)
        low0 = plus(p10 + from_low)
        high1 = minus(p31 + from_high)
        keep = p00 + low0 + high0
        give = p01 + low1 + high1
        projected = keep + far(give)
        start_first = jnp.where(fresh, F32(0.0), first_t[:, a : a + n])
        start_second = jnp.where(fresh, F32(0.0), second_t[:, a : a + n])
        new_first = BETA_ONE * start_first + (1.0 - BETA_ONE) * projected
        new_second = BETA_TWO * start_second + (1.0 - BETA_TWO) * projected * projected
        ratio = (new_first / (jnp.sqrt(new_second) + ADAM_EPS)).astype(BF16)
        firsts.append(new_first)
        seconds.append(new_second)
        ratios.append(ratio)

    weight = None
    total = jnp.zeros((2 * hidden.shape[0], old_weight.shape[1]), F32)
    for (a, n), r0 in zip(cuts, ratios):
        rz = far(r0)
        m0 = plus(r0)
        q0 = minus(r0)
        t0 = plus(m0)
        mz = plus(rz)
        qz = minus(rz)
        tz = minus(qz)
        mine = jnp.concatenate([r0, rz, q0, qz, t0, tz, m0, mz], axis=0)
        theirs = twin(mine)
        weight, total = update(
            weight, mine, theirs, basis_own, basis_send, old_weight, hidden, hid_far, total, a, n
        )

    seqs = hidden.shape[0]
    near, away = total[:seqs], twin(total[seqs:])
    d = lax.axis_index("dp")
    pair = jnp.where(d == 0, jnp.stack([near, away]), jnp.stack([away, near]))
    cols = frame_basis.shape[0] // 8
    parts = pair.reshape(2, seqs, 8, cols).transpose(0, 2, 1, 3).reshape(16, seqs * cols // 128, 128)
    got = lax.all_to_all(parts, "tp", 0, 0, tiled=True)
    mlp_out = jnp.sum(got, axis=0).reshape(seqs, cols).astype(BF16)
    return (
        jnp.concatenate(firsts, axis=1).T,
        jnp.concatenate(seconds, axis=1).T,
        weight,
        mlp_out,
    )


def solution(mesh):
    placed = (
        P("tp", ("learn", "dp")),
        P(("learn", "dp"), None),
        P("tp", ("learn", "dp")),
        P("tp", ("learn", "dp")),
        P(("learn", "dp")),
        P("tp", ("learn", "dp")),
        P("dp", "tp"),
    )
    return jax.shard_map(
        shards,
        mesh=mesh,
        in_specs=placed,
        out_specs=(
            P("tp", ("learn", "dp")),
            P("tp", ("learn", "dp")),
            P("tp", ("learn", "dp")),
            P("dp", ("learn", "tp")),
        ),
        check_vma=False,
    )
```

```python
import functools

import jax
import jax.numpy as jnp
from jax import lax
from jax.experimental import pallas as pl
from jax.experimental.pallas import tpu as pltpu
from jax.sharding import PartitionSpec as P

BETA_ONE = 0.9
BETA_TWO = 0.999
ADAM_EPS = 1e-06
STEP_RATE = 0.01
RING = 4
ROWS = 384
VMEM = 16 * 2**20
F32 = jnp.float32
BF16 = jnp.bfloat16
SHAPE = jax.ShapeDtypeStruct
ORDER = (0, 1, 3, 2)


WHOLE = pl.BlockSpec(memory_space=pltpu.VMEM)
ANYWHERE = pl.BlockSpec(memory_space=pl.ANY)


def call(kernel, out_shape, args, in_specs=None, out_specs=None, grid=(), deps=(), held=(), scratch=()):
    n_in, n_out, n_held = len(args), len(out_shape), len(held)

    def body(*refs):
        rest = refs[n_in + n_held + len(deps) :]
        kernel(*refs[:n_in], *rest[:n_out], *rest[n_out + n_held :])

    specs = list(in_specs or [WHOLE] * n_in)
    args = [pltpu.with_memory_space_constraint(a, pltpu.VMEM) if s is WHOLE else a for a, s in zip(args, specs)]
    out_specs = list(out_specs or [WHOLE] * n_out)
    out_shape = [pltpu.VMEM(o.shape, o.dtype) if s is WHOLE else o for o, s in zip(out_shape, out_specs)]

    return pl.pallas_call(
        body,
        grid=grid,
        in_specs=specs + [ANYWHERE] * (n_held + len(deps)),
        out_specs=out_specs + [ANYWHERE] * n_held,
        out_shape=list(out_shape) + [SHAPE(h.shape, h.dtype) for h in held],
        scratch_shapes=list(scratch),
        input_output_aliases={n_in + i: n_out + i for i in range(n_held)},
        compiler_params=pltpu.CompilerParams(vmem_limit_bytes=VMEM),
        cost_estimate=pl.CostEstimate(flops=0, bytes_accessed=0, transcendentals=0),
    )(*args, *held, *deps)


def arrange_kernel(where_ref, basis_ref, all_ref, send_ref, turned):
    zh, x, d = where_ref[0], where_ref[1], where_ref[2]
    width = turned.shape[0] // 16
    turned[...] = basis_ref[...].T
    for side in range(2):
        for place, j in enumerate(ORDER):
            for zrel in range(2):
                block = ((zh ^ zrel) * RING + ((x + j) & (RING - 1))) * 2 + (d ^ side)
                rows = turned[pl.ds(pl.multiple_of(block * width, width), width), :]
                first = (RING * zrel + place) * width
                if side == 1:
                    send_ref[first : first + width, :] = rows
                first += side * 8 * width
                all_ref[first : first + width, :] = rows


def arrange(where, basis):
    depth, rank = basis.shape
    return pl.pallas_call(
        arrange_kernel,
        grid_spec=pltpu.PrefetchScalarGridSpec(
            num_scalar_prefetch=1,
            grid=(1,),
            in_specs=[pl.BlockSpec((depth, rank), lambda i, w: (0, 0))],
            out_specs=[
                pl.BlockSpec((rank, depth), lambda i, w: (0, 0)),
                pl.BlockSpec((rank // 2, depth), lambda i, w: (0, 0)),
            ],
            scratch_shapes=[pltpu.VMEM((rank, depth), basis.dtype)],
        ),
        out_shape=(SHAPE((rank, depth), basis.dtype), SHAPE((rank // 2, depth), basis.dtype)),
        compiler_params=pltpu.CompilerParams(vmem_limit_bytes=VMEM),
        cost_estimate=pl.CostEstimate(flops=0, bytes_accessed=0, transcendentals=0),
    )(where, basis)


def chunks(rows):
    return [(at, min(ROWS, rows - at)) for at in range(0, rows, ROWS)]


def project_kernel(zrel, own_ref, other_ref, mine_ref, theirs_ref, up_out, down_out, up2_out, down2_out, own_out):
    contract = (((1,), (1,)), ((), ()))
    w = own_out.shape[0]
    h = w // 2
    ranks = slice(zrel * RING * w, (zrel + 1) * RING * w)
    for at, n in chunks(mine_ref.shape[0]):
        rows = slice(at, at + n)
        low = lax.dot_general(own_ref[ranks, :], mine_ref[rows, :], contract, preferred_element_type=F32)
        low += lax.dot_general(other_ref[ranks, :], theirs_ref[rows, :], contract, preferred_element_type=F32)
        own, above, below, two = (low[w * k : w * (k + 1)] for k in range(RING))
        up_out[:h, rows] = two[:h]
        up_out[h:, rows] = above[h:]
        down_out[:h, rows] = two[h:]
        down_out[h:, rows] = below[:h]
        up2_out[:, rows] = above[:h]
        down2_out[:, rows] = below[h:]
        own_out[:, rows] = own


def project(basis_all, basis_recv, gradient, theirs, zrel, count, deps=()):
    w = basis_recv.shape[0] // 8
    heights = (w, w, w // 2, w // 2, w)
    return call(
        functools.partial(project_kernel, zrel),
        [SHAPE((h, count), F32) for h in heights],
        (basis_all, basis_recv, gradient, theirs),
        deps=deps,
    )


def hop_kernel(up_ref, down_ref, below_ref, above_ref, up_out, down_out):
    h = up_ref.shape[0]
    up_out[...] = up_ref[...] + below_ref[:h, :]
    down_out[...] = down_ref[...] + above_ref[:h, :]


def hop(low, below, above, deps=()):
    shape = SHAPE(low[2].shape, F32)
    return call(hop_kernel, [shape, shape], (low[2], low[3], below, above), deps=deps)


def settle_kernel(own_ref, below_ref, above_ref, below2_ref, above2_ref, out_ref):
    h = below2_ref.shape[0]
    out_ref[:h, :] = own_ref[:h, :] + above_ref[h:, :] + below2_ref[...]
    out_ref[h:, :] = own_ref[h:, :] + below_ref[h:, :] + above2_ref[...]


def settle(low, first, second, held=()):
    return call(settle_kernel, [SHAPE(low[4].shape, F32)], (low[4], *first, *second), held=held)


def moment_step(sum_ref, came_ref, fresh_ref, first_ref, second_ref):
    here = slice(0, first_ref.shape[1])
    projected = sum_ref[:, here] + came_ref[:, here]
    fresh = fresh_ref[...] == 1
    start_first = jnp.where(fresh, F32(0.0), first_ref[...])
    start_second = jnp.where(fresh, F32(0.0), second_ref[...])
    new_first = BETA_ONE * start_first + (1.0 - BETA_ONE) * projected
    new_second = BETA_TWO * start_second + (1.0 - BETA_TWO) * projected * projected
    return new_first, new_second


def ratio_kernel(*refs):
    new_first, new_second = moment_step(*refs[:-1])
    refs[-1][:, : new_first.shape[1]] = (new_first / (jnp.sqrt(new_second) + ADAM_EPS)).astype(BF16)


def moments_kernel(*refs):
    refs[-2][...], refs[-1][...] = moment_step(*refs[:-2])


def hold(values, *deps):
    return call(lambda *refs: None, [], (), held=values, deps=deps)


def update_kernel(parts, *refs):
    basis_ref, old_ref, hid_ref, hid_far_ref, new_ref, out_ref, ratio = refs[parts:]
    at = 0
    for ref in refs[:parts]:
        ratio[at : at + ref.shape[0], :] = ref[...]
        at += ref.shape[0]
    contract = (((0,), (0,)), ((), ()))
    for at, n in chunks(old_ref.shape[0]):
        rows = slice(at, at + n)
        delta = lax.dot_general(ratio[:, rows], basis_ref[...], contract, preferred_element_type=F32)
        new = (old_ref[rows, :].astype(F32) - STEP_RATE * delta).astype(BF16)
        new_ref[rows, :] = new
        hid = jnp.concatenate([hid_ref[:, rows], hid_far_ref[:, rows]], axis=0)
        term = jnp.dot(hid, new, preferred_element_type=F32)
        if at == 0:
            out_ref[...] = term
        else:
            out_ref[...] += term


def update(ratios, basis_all, old, hid, hid_far):
    ranks, depth = basis_all.shape
    return call(
        functools.partial(update_kernel, len(ratios)),
        [SHAPE(old.shape, BF16), SHAPE((2 * hid.shape[0], depth), F32)],
        (*ratios, basis_all, old, hid, hid_far),
        scratch=[pltpu.VMEM((ranks, ratios[0].shape[1]), BF16)],
    )


def shards(gradient, frame_basis, moment_first, moment_second, refresh, old_weight, hidden):
    learn = lax.axis_index("learn")
    where = jnp.stack([learn // RING, learn % RING, lax.axis_index("dp")]).astype(jnp.int32)
    up = [(z * RING + x, z * RING + (x + 1) % RING) for z in range(2) for x in range(RING)]
    down = [(b, a) for a, b in up]
    across = [(i, (i + RING) % (2 * RING)) for i in range(2 * RING)]
    twice = [(z * RING + x, z * RING + (x + 2) % RING) for z in range(2) for x in range(RING)]
    plus = lambda v: lax.ppermute(v, "learn", up)
    minus = lambda v: lax.ppermute(v, "learn", down)
    far = lambda v: lax.ppermute(v, "learn", across)
    two_away = lambda v: lax.ppermute(v, "learn", twice)
    twin = lambda v: lax.ppermute(v, "dp", [(0, 1), (1, 0)])

    rows, depth = gradient.shape
    count = -(-rows // 128) * 128

    theirs = twin(gradient)
    basis_all, basis_send = arrange(where, frame_basis)
    basis_recv = twin(basis_send)
    hid_far = twin(hidden)
    fresh = refresh[:, None]

    give = project(basis_all, basis_recv, gradient, theirs, 1, count)
    give_got = plus(give[0]), minus(give[1])
    keep = project(basis_all, basis_recv, gradient, theirs, 0, count, deps=(give[0],))
    give_send = hop(give, *give_got, deps=(keep[0],))
    give_got2 = plus(give_send[0]), minus(give_send[1])
    given, *keep_held = settle(give, give_got, give_got2, keep[:2])
    came = far(given)
    keep_got = plus(keep_held[0]), minus(keep_held[1])
    keep_send = hop(keep, *keep_got)
    keep_got2 = plus(keep_send[0]), minus(keep_send[1])
    kept = settle(keep, keep_got, keep_got2)[0]
    args = (kept, came, fresh, moment_first.T, moment_second.T)
    r = call(ratio_kernel, [SHAPE(kept.shape, BF16)], args)[0]

    rz = far(r)
    below, above, opposite = plus(r), minus(r), two_away(r)
    new_first, new_second = call(moments_kernel, [SHAPE(moment_first.T.shape, F32)] * 2, args, deps=(r,))
    (rz,) = hold((rz,), below, above, opposite, hid_far, new_first)
    below_z, above_z = plus(rz), minus(rz)
    ratios = (r, above, below, opposite, rz, above_z, below_z, two_away(rz))
    others = [twin(v) for v in ratios]
    weight, total = update((*ratios, *others), basis_all, old_weight, hidden, hid_far)

    seqs = hidden.shape[0]
    here, there = total[:seqs], twin(total[seqs:])
    d = lax.axis_index("dp")
    pair = jnp.where(d == 0, jnp.stack([here, there]), jnp.stack([there, here]))
    cols = depth // 8
    parts = pair.reshape(2, seqs, 8, cols).transpose(0, 2, 1, 3).reshape(16, seqs * cols // 128, 128)
    got = lax.all_to_all(parts.astype(BF16), "tp", 0, 0, tiled=True)
    mlp_out = jnp.sum(got.astype(F32), axis=0).reshape(seqs, cols).astype(BF16)
    return new_first.T, new_second.T, weight, mlp_out


def solution(mesh):
    placed = (
        P("tp", ("learn", "dp")),
        P(("learn", "dp"), None),
        P("tp", ("learn", "dp")),
        P("tp", ("learn", "dp")),
        P(("learn", "dp")),
        P("tp", ("learn", "dp")),
        P("dp", "tp"),
    )
    return jax.shard_map(
        shards,
        mesh=mesh,
        in_specs=placed,
        out_specs=(
            P("tp", ("learn", "dp")),
            P("tp", ("learn", "dp")),
            P("tp", ("learn", "dp")),
            P("dp", ("learn", "tp")),
        ),
        check_vma=False,
    )
```

```python
import functools

import jax
import jax.numpy as jnp
from jax import lax
from jax.experimental import pallas as pl
from jax.experimental.pallas import tpu as pltpu
from jax.sharding import PartitionSpec as P

BETA_ONE = 0.9
BETA_TWO = 0.999
ADAM_EPS = 1e-06
STEP_RATE = 0.01
RING = 4
ROWS = 1024
VMEM = 16 * 2**20
F32 = jnp.float32
BF16 = jnp.bfloat16
SHAPE = jax.ShapeDtypeStruct
ORDER = (0, 1, 3, 2)


WHOLE = pl.BlockSpec(memory_space=pltpu.VMEM)
ANYWHERE = pl.BlockSpec(memory_space=pl.ANY)


def call(kernel, out_shape, args, in_specs=None, out_specs=None, grid=(), deps=(), held=(), scratch=()):
    n_in, n_out, n_held = len(args), len(out_shape), len(held)

    def body(*refs):
        rest = refs[n_in + n_held + len(deps) :]
        kernel(*refs[:n_in], *rest[:n_out], *rest[n_out + n_held :])

    specs = list(in_specs or [WHOLE] * n_in)
    args = [pltpu.with_memory_space_constraint(a, pltpu.VMEM) if s is WHOLE else a for a, s in zip(args, specs)]
    out_specs = list(out_specs or [WHOLE] * n_out)
    out_shape = [pltpu.VMEM(o.shape, o.dtype) if s is WHOLE else o for o, s in zip(out_shape, out_specs)]

    return pl.pallas_call(
        body,
        grid=grid,
        in_specs=specs + [ANYWHERE] * (n_held + len(deps)),
        out_specs=out_specs + [ANYWHERE] * n_held,
        out_shape=list(out_shape) + [SHAPE(h.shape, h.dtype) for h in held],
        scratch_shapes=list(scratch),
        input_output_aliases={n_in + i: n_out + i for i in range(n_held)},
        compiler_params=pltpu.CompilerParams(vmem_limit_bytes=VMEM),
        cost_estimate=pl.CostEstimate(flops=0, bytes_accessed=0, transcendentals=0),
    )(*args, *held, *deps)


def arrange_kernel(where_ref, basis_ref, all_ref, send_ref, turned):
    zh, x, d = where_ref[0], where_ref[1], where_ref[2]
    width = turned.shape[0] // 16
    turned[...] = basis_ref[...].T
    for side in range(2):
        for place, j in enumerate(ORDER):
            for zrel in range(2):
                block = ((zh ^ zrel) * RING + ((x + j) & (RING - 1))) * 2 + (d ^ side)
                rows = turned[pl.ds(pl.multiple_of(block * width, width), width), :]
                first = (RING * zrel + place) * width
                if side == 1:
                    send_ref[first : first + width, :] = rows
                first += side * 8 * width
                all_ref[first : first + width, :] = rows


def arrange(where, basis):
    depth, rank = basis.shape
    return pl.pallas_call(
        arrange_kernel,
        grid_spec=pltpu.PrefetchScalarGridSpec(
            num_scalar_prefetch=1,
            grid=(1,),
            in_specs=[pl.BlockSpec((depth, rank), lambda i, w: (0, 0))],
            out_specs=[
                pl.BlockSpec((rank, depth), lambda i, w: (0, 0)),
                pl.BlockSpec((rank // 2, depth), lambda i, w: (0, 0)),
            ],
            scratch_shapes=[pltpu.VMEM((rank, depth), basis.dtype)],
        ),
        out_shape=(SHAPE((rank, depth), basis.dtype), SHAPE((rank // 2, depth), basis.dtype)),
        compiler_params=pltpu.CompilerParams(vmem_limit_bytes=VMEM),
        cost_estimate=pl.CostEstimate(flops=0, bytes_accessed=0, transcendentals=0),
    )(where, basis)


def chunks(rows):
    return [(at, min(ROWS, rows - at)) for at in range(0, rows, ROWS)]


def project_kernel(zrel, own_ref, other_ref, mine_ref, theirs_ref, up_out, down_out, up2_out, down2_out, own_out):
    contract = (((1,), (1,)), ((), ()))
    w = own_out.shape[0]
    h = w // 2
    ranks = slice(zrel * RING * w, (zrel + 1) * RING * w)
    for at, n in chunks(mine_ref.shape[0]):
        rows = slice(at, at + n)
        low = lax.dot_general(own_ref[ranks, :], mine_ref[rows, :], contract, preferred_element_type=F32)
        low += lax.dot_general(other_ref[ranks, :], theirs_ref[rows, :], contract, preferred_element_type=F32)
        own, above, below, two = (low[w * k : w * (k + 1)] for k in range(RING))
        up_out[:h, rows] = two[:h]
        up_out[h:, rows] = above[h:]
        down_out[:h, rows] = two[h:]
        down_out[h:, rows] = below[:h]
        up2_out[:, rows] = above[:h]
        down2_out[:, rows] = below[h:]
        own_out[:, rows] = own


def project(basis_all, basis_recv, gradient, theirs, zrel, count, deps=()):
    w = basis_recv.shape[0] // 8
    heights = (w, w, w // 2, w // 2, w)
    return call(
        functools.partial(project_kernel, zrel),
        [SHAPE((h, count), F32) for h in heights],
        (basis_all, basis_recv, gradient, theirs),
        deps=deps,
    )


def hop_kernel(up_ref, down_ref, below_ref, above_ref, up_out, down_out):
    h = up_ref.shape[0]
    up_out[...] = up_ref[...] + below_ref[:h, :]
    down_out[...] = down_ref[...] + above_ref[:h, :]


def hop(low, below, above, deps=()):
    shape = SHAPE(low[2].shape, F32)
    return call(hop_kernel, [shape, shape], (low[2], low[3], below, above), deps=deps)


def settle_kernel(own_ref, below_ref, above_ref, below2_ref, above2_ref, out_ref):
    h = below2_ref.shape[0]
    out_ref[:h, :] = own_ref[:h, :] + above_ref[h:, :] + below2_ref[...]
    out_ref[h:, :] = own_ref[h:, :] + below_ref[h:, :] + above2_ref[...]


def settle(low, first, second, held=()):
    return call(settle_kernel, [SHAPE(low[4].shape, F32)], (low[4], *first, *second), held=held)


def moment_step(sum_ref, came_ref, fresh_ref, first_ref, second_ref):
    here = slice(0, first_ref.shape[1])
    projected = sum_ref[:, here] + came_ref[:, here]
    fresh = fresh_ref[...] == 1
    start_first = jnp.where(fresh, F32(0.0), first_ref[...])
    start_second = jnp.where(fresh, F32(0.0), second_ref[...])
    new_first = BETA_ONE * start_first + (1.0 - BETA_ONE) * projected
    new_second = BETA_TWO * start_second + (1.0 - BETA_TWO) * projected * projected
    return new_first, new_second


def ratio_kernel(*refs):
    new_first, new_second = moment_step(*refs[:-1])
    refs[-1][:, : new_first.shape[1]] = (new_first / (jnp.sqrt(new_second) + ADAM_EPS)).astype(BF16)


def moments_kernel(*refs):
    refs[-2][...], refs[-1][...] = moment_step(*refs[:-2])


def hold(values, *deps):
    return call(lambda *refs: None, [], (), held=values, deps=deps)


def update_kernel(parts, *refs):
    basis_ref, old_ref, hid_ref, hid_far_ref, new_ref, out_ref, ratio = refs[parts:]
    at = 0
    for ref in refs[:parts]:
        ratio[at : at + ref.shape[0], :] = ref[...]
        at += ref.shape[0]
    contract = (((0,), (0,)), ((), ()))
    for at, n in chunks(old_ref.shape[0]):
        rows = slice(at, at + n)
        delta = lax.dot_general(ratio[:, rows], basis_ref[...], contract, preferred_element_type=F32)
        new = (old_ref[rows, :].astype(F32) - STEP_RATE * delta).astype(BF16)
        new_ref[rows, :] = new
        hid = jnp.concatenate([hid_ref[:, rows], hid_far_ref[:, rows]], axis=0)
        term = jnp.dot(hid, new, preferred_element_type=F32)
        if at == 0:
            out_ref[...] = term
        else:
            out_ref[...] += term


def update(ratios, basis_all, old, hid, hid_far):
    ranks, depth = basis_all.shape
    return call(
        functools.partial(update_kernel, len(ratios)),
        [SHAPE(old.shape, BF16), SHAPE((2 * hid.shape[0], depth), F32)],
        (*ratios, basis_all, old, hid, hid_far),
        scratch=[pltpu.VMEM((ranks, ratios[0].shape[1]), BF16)],
    )


def shards(gradient, frame_basis, moment_first, moment_second, refresh, old_weight, hidden):
    learn = lax.axis_index("learn")
    where = jnp.stack([learn // RING, learn % RING, lax.axis_index("dp")]).astype(jnp.int32)
    up = [(z * RING + x, z * RING + (x + 1) % RING) for z in range(2) for x in range(RING)]
    down = [(b, a) for a, b in up]
    across = [(i, (i + RING) % (2 * RING)) for i in range(2 * RING)]
    twice = [(z * RING + x, z * RING + (x + 2) % RING) for z in range(2) for x in range(RING)]
    plus = lambda v: lax.ppermute(v, "learn", up)
    minus = lambda v: lax.ppermute(v, "learn", down)
    far = lambda v: lax.ppermute(v, "learn", across)
    two_away = lambda v: lax.ppermute(v, "learn", twice)
    twin = lambda v: lax.ppermute(v, "dp", [(0, 1), (1, 0)])

    rows, depth = gradient.shape
    count = -(-rows // 128) * 128

    theirs = twin(gradient)
    basis_all, basis_send = arrange(where, frame_basis)
    basis_recv = twin(basis_send)
    hid_far = twin(hidden)
    fresh = refresh[:, None]

    give = project(basis_all, basis_recv, gradient, theirs, 1, count)
    give_got = plus(give[0]), minus(give[1])
    keep = project(basis_all, basis_recv, gradient, theirs, 0, count, deps=(give[0],))
    give_send = hop(give, *give_got, deps=(keep[0],))
    give_got2 = plus(give_send[0]), minus(give_send[1])
    given, *keep_held = settle(give, give_got, give_got2, keep[:2])
    came = far(given)
    keep_got = plus(keep_held[0]), minus(keep_held[1])
    keep_send = hop(keep, *keep_got)
    keep_got2 = plus(keep_send[0]), minus(keep_send[1])
    kept = settle(keep, keep_got, keep_got2)[0]
    args = (kept, came, fresh, moment_first.T, moment_second.T)
    r = call(ratio_kernel, [SHAPE(kept.shape, BF16)], args)[0]

    rz = far(r)
    below, above, opposite = plus(r), minus(r), two_away(r)
    new_first, new_second = call(moments_kernel, [SHAPE(moment_first.T.shape, F32)] * 2, args, deps=(r,))
    (rz,) = hold((rz,), below, above, opposite, hid_far, new_first)
    below_z, above_z = plus(rz), minus(rz)
    ratios = (r, above, below, opposite, rz, above_z, below_z, two_away(rz))
    others = [twin(v) for v in ratios]
    weight, total = update((*ratios, *others), basis_all, old_weight, hidden, hid_far)

    seqs = hidden.shape[0]
    here, there = total[:seqs], twin(total[seqs:])
    d = lax.axis_index("dp")
    pair = jnp.where(d == 0, jnp.stack([here, there]), jnp.stack([there, here]))
    cols = depth // 8
    parts = pair.reshape(2, seqs, 8, cols).transpose(0, 2, 1, 3).reshape(16, seqs * cols // 128, 128)
    got = lax.all_to_all(parts.astype(BF16), "tp", 0, 0, tiled=True)
    mlp_out = jnp.sum(got.astype(F32), axis=0).reshape(seqs, cols).astype(BF16)
    return new_first.T, new_second.T, weight, mlp_out


def solution(mesh):
    placed = (
        P("tp", ("learn", "dp")),
        P(("learn", "dp"), None),
        P("tp", ("learn", "dp")),
        P("tp", ("learn", "dp")),
        P(("learn", "dp")),
        P("tp", ("learn", "dp")),
        P("dp", "tp"),
    )
    return jax.shard_map(
        shards,
        mesh=mesh,
        in_specs=placed,
        out_specs=(
            P("tp", ("learn", "dp")),
            P("tp", ("learn", "dp")),
            P("tp", ("learn", "dp")),
            P("dp", ("learn", "tp")),
        ),
        check_vma=False,
    )
```
